32 devices in a mesh: group: 2 (over y), row: 4 (over z), head: 2 (over x), sub: 2 (over core).
Axes of the slice: x: 2, y: 2, z: 4, core: 2. Of those that a mesh axis runs over, the one named last changes fastest.
Arguments:
- prior_state: float32 [64, 32, 128, 128], P(('group', 'row'), 'head', None, 'sub'), parts along dimension 0, may hold values from -6 to 6
- queries: bfloat16 [2, 64, 32, 128], P(None, ('group', 'row'), 'head'), parts along dimension 1, may hold values from -6 to 6
- new_keys: bfloat16 [2, 64, 32, 128], P(None, ('group', 'row'), 'head'), parts along dimension 1, may hold values from -6 to 6
- new_values: bfloat16 [2, 64, 32, 128], P(None, ('group', 'row'), 'head', 'sub'), parts along dimension 1, may hold values from -6 to 6
- out_gates: bfloat16 [2, 64, 32, 128], P(None, ('group', 'row'), 'head', 'sub'), parts along dimension 1, may hold values from -6 to 6
- decay_rates: float32 [32], P('head'), may hold values from 0.3 to 0.98
- norm_gain: float32 [32, 128], P('head', 'sub'), may hold values from 0.1 to 1.9
- out_weight: bfloat16 [32, 128, 3072], P('head', 'sub'), may hold values from -0.09375 to 0.09375
- residual: bfloat16 [2, 64, 3072], P(None, ('group', 'row')), parts along dimension 1, may hold values from -4 to 4
- ffn_gain: float32 [3072], replicated, may hold values from 0.1 to 1.9
- router_weight: bfloat16 [3072, 4], replicated, may hold values from -0.109375 to 0.109375
- gate_weight: bfloat16 [3072, 32768], P(None, ('row', 'head', 'sub')), may hold values from -0.109375 to 0.109375
- up_weight: bfloat16 [3072, 32768], P(None, ('row', 'head', 'sub')), may hold values from -0.109375 to 0.109375
- down_weight: bfloat16 [32768, 3072], P(('row', 'head', 'sub')), may hold values from -0.0625 to 0.0625
- expert_picks: int32 [2, 64, 2], P(None, ('group', 'row')), parts along dimension 1, may hold values from 0 to 3, all different within a row; in each aligned block of 8 rows (0 to 7, 8 to 15, ..., all dimensions but the last counted through in order) at most 6 rows name the same one
- finished: int32 [2, 64], P(None, ('group', 'row')), parts along dimension 1, may hold values from 0 to 1, as said below
- dest_slots: int32 [2, 64], P(None, ('group', 'row')), parts along dimension 1, may hold values from 0 to 31, as said below
Outputs:
- layer_out: bfloat16 [2, 64, 3072], P(None, ('group', 'row'), ('head', 'sub')), parts along dimension 1
The draws below stay inside these ranges and needn't reach their ends.
There are 2 independent parts, one for each index of `group`. The reference program is written for one: setup_inputs(seed, part) draws one part's arguments, and reference() takes and returns one part's arrays. A program takes and returns all parts, laid end to end along the dimension named above; an argument that names none is the same for every part. Nothing has to cross between parts.
Inputs may be any that keep to these rules, and one draw needn't show every extreme that they name: `expert_picks`: in each step, the rows of one index of row name one expert at most 6 times, and the two picks of a row differ. A row finished at the first step is finished at the second. `dest_slots`: for each step a permutation of the rows of the group; rows that are not finished take the lowest slots.
All inputs are finite; a program needn't handle non-finite values.
Results may differ from the reference program's by a relative error of at most 0.0063.
Values may be sent and summed in bfloat16 or wider, within the bound.
A program may use at most 128 MiB of HBM per device.

```python
import math
import jax
import jax.numpy as jnp
import numpy as np
from jax import lax

D = 3072
HEADS = 32
HEAD_DIM = 128
FF = 8192
EXPERTS = 4
TOP = 2
STEPS = 2
ROW_DEV = 8
CAP = 6
ROWS = 32


def finished_flags(key):
    first_key = jax.random.fold_in(key, 101)
    later_key = jax.random.fold_in(key, 102)
    first_done = jax.random.randint(first_key, (ROWS,), 0, 5) == 0
    later_done = jax.random.randint(later_key, (ROWS,), 0, 5) == 0
    second_done = jnp.logical_or(first_done, later_done)
    return jnp.stack([first_done, second_done], axis=0).astype(jnp.int32)


def draw_finished(key, part):
    key = jax.random.fold_in(key, 3)
    return finished_flags(key)[:STEPS]


def draw_dest_slots(key, part):
    flags = finished_flags(jax.random.fold_in(key, 3))[:STEPS]
    key = jax.random.fold_in(key, 5)
    result = []
    for step_index in range(STEPS):
        ranks = jax.random.permutation(jax.random.fold_in(key, step_index), ROWS).astype(jnp.int32)
        scores = flags[step_index] * ROWS + ranks
        order = jnp.argsort(scores, stable=True).astype(jnp.int32)
        result.append(jnp.argsort(order, stable=True).astype(jnp.int32))
    return jnp.stack(result, axis=0)


def steps_of(stream_key, shape, shards, least, high):
    def one(axis_at, shards_of):
        heights = jax.random.uniform(jax.random.fold_in(jax.random.fold_in(stream_key, 6), axis_at), (shards_of,), jnp.float32, least / len(shards), high / len(shards))
        return jnp.repeat(jnp.exp(heights), shape[axis_at] // shards_of).reshape((-1,) + (1,) * (len(shape) - axis_at - 1))

    factor_of = one(*shards[0])
    for cut in shards[1:]:
        factor_of = factor_of * one(*cut)
    return factor_of


def deal_out(rng, own, number, rows, amount, top, most, slope):
    sequence = jax.random.permutation(rng, amount)
    crowded, common = portions_of(amount, rows * top, most, slope, True), portions_of(amount, rows * top, most, slope, False)
    places = jnp.arange(amount)

    def named(tallies, offset_by):
        used = int((tallies > 0).sum())
        fixed = max(1, used // 4)
        moved = fixed + (places - fixed + offset_by * (used - fixed)) % max(1, amount - fixed)
        return jnp.zeros((amount,), jnp.int32).at[sequence[jnp.where(places < fixed, places, moved)]].set(jnp.asarray(tallies, jnp.int32))

    tallies = jnp.where(number % 4 == 0, named(crowded, number // 4), named(common, number - number // 4 - 1))
    mixed = jax.random.permutation(jax.random.fold_in(own, 3), amount)
    source_of, receiver = mixed[0:amount // 2 * 2:2], mixed[1:amount // 2 * 2:2]
    margin = jnp.minimum(tallies[source_of] - 1, most - tallies[receiver]) // 2
    margin = jnp.where((source_of == sequence[0]) | (receiver == sequence[0]) | (tallies[receiver] == 0), 0, jnp.maximum(margin, 0))
    moved = jax.random.randint(jax.random.fold_in(own, 4), (amount // 2,), 0, 1 << 20) % (margin + 1)
    tallies = tallies.at[source_of].add(-moved).at[receiver].add(moved)
    members = jnp.searchsorted(jnp.cumsum(tallies), jnp.arange(rows * top), side="right").astype(jnp.int32)
    grid = members.reshape(top, rows).T
    grid = grid[jax.random.permutation(jax.random.fold_in(own, 1), rows)]
    offset_by = jax.random.randint(jax.random.fold_in(own, 2), (rows, 1), 0, top)
    return jnp.take_along_axis(grid, (jnp.arange(top)[None, :] + offset_by) % top, axis=1)


def portions_of(amount, total, bound, slope, full):
    weights = [(1 << 20) // math.isqrt(standing ** slope) + 1 for standing in range(1, amount + 1)]
    largest = bound if full else min(bound, max(-(-total // amount), total * weights[0] // sum(weights)))
    least = 1 if total - largest >= amount - 1 else 0
    holding, rest = [largest] + [least] * (amount - 1), total - largest - least * (amount - 1)
    while rest > 0:
        movable = [i for i in range(1, amount) if holding[i] < largest] or [i for i in range(1, amount) if holding[i] < bound]
        mass, remaining = sum([weights[i] for i in movable]), rest
        for i in movable:
            extra = min(bound - holding[i], max(1, remaining * weights[i] // mass), rest)
            holding[i] = holding[i] + extra
            rest = rest - extra
    return np.array(holding)


def centred(rng, shape, scale, reach, pieces=(), kind=jnp.bfloat16):
    level = steps_of(rng, shape, pieces, -0.22, 0.18) if pieces else 1.0
    values = jax.random.normal(rng, shape, jnp.float32) * scale * level
    return jnp.minimum(jnp.maximum(values, -reach), reach).astype(kind)


def setup_inputs(seed: int = 0, part: int = 0) -> dict:
    seeds = jax.random.split(jax.random.key(seed), 18)
    part_splits = jax.random.split(jax.random.fold_in(seeds[17], part), 18)
    prior_state = centred(part_splits[0], (ROWS, HEADS, HEAD_DIM, HEAD_DIM), 1.0, 6.0, ((0, 4), (1, 2), (3, 2)), jnp.float32)
    queries = centred(part_splits[1], (STEPS, ROWS, HEADS, HEAD_DIM), 1.0, 6.0, ((1, 4), (2, 2)))
    new_keys = centred(part_splits[2], (STEPS, ROWS, HEADS, HEAD_DIM), 1.0, 6.0, ((1, 4), (2, 2)))
    new_values = centred(part_splits[3], (STEPS, ROWS, HEADS, HEAD_DIM), 1.0, 6.0, ((1, 4), (2, 2), (3, 2)))
    out_gates = centred(part_splits[4], (STEPS, ROWS, HEADS, HEAD_DIM), 1.5, 6.0, ((1, 4), (2, 2), (3, 2)))
    decay_rates = jnp.clip(jnp.exp(math.log(0.98) - 1.1837701 * jax.random.uniform(seeds[5], (HEADS,), jnp.float32) ** steps_of(seeds[5], (HEADS,), ((0, 2),), -0.2, 0.2)), 0.3, 0.98)
    norm_gain = jnp.clip(1.0 + 0.18 * jax.random.normal(seeds[6], (HEADS, HEAD_DIM), jnp.float32), 0.1, 1.9)
    out_weight = centred(seeds[7], (HEADS, HEAD_DIM, D), (HEADS * HEAD_DIM) ** -0.5, 0.09375, ((0, 2), (1, 2)))
    residual = centred(part_splits[8], (STEPS, ROWS, D), 0.5, 4.0, ((1, 4),))
    ffn_gain = jnp.clip(1.0 + 0.18 * jax.random.normal(seeds[9], (D,), jnp.float32), 0.1, 1.9)
    router_weight = centred(seeds[10], (D, EXPERTS), D ** -0.5, 0.109375)
    gate_weight = centred(seeds[11], (D, EXPERTS * FF), D ** -0.5, 0.109375, ((1, 16),))
    up_weight = centred(seeds[12], (D, EXPERTS * FF), D ** -0.5, 0.109375, ((1, 16),))
    down_weight = centred(seeds[13], (EXPERTS * FF, D), FF ** -0.5, 0.0625, ((0, 16),))
    expert_picks_keys = jax.random.split(jax.random.fold_in(part_splits[14], 1), STEPS * ROWS // ROW_DEV)
    expert_picks_turns = jax.random.permutation(jax.random.fold_in(part_splits[14], 3), STEPS * ROWS // ROW_DEV)
    expert_picks = jax.vmap(lambda own, number: deal_out(jax.random.fold_in(part_splits[14], 2), own, number, ROW_DEV, EXPERTS, TOP, CAP, 2))(expert_picks_keys, expert_picks_turns).reshape((STEPS, ROWS, TOP))
    finished = draw_finished(jax.random.fold_in(jax.random.fold_in(seeds[17], part), 71), part)
    dest_slots = draw_dest_slots(jax.random.fold_in(jax.random.fold_in(seeds[17], part), 71), part)
    return {"prior_state": prior_state, "queries": queries, "new_keys": new_keys, "new_values": new_values, "out_gates": out_gates, "decay_rates": decay_rates, "norm_gain": norm_gain, "out_weight": out_weight, "residual": residual, "ffn_gain": ffn_gain, "router_weight": router_weight, "gate_weight": gate_weight, "up_weight": up_weight, "down_weight": down_weight, "expert_picks": expert_picks, "finished": finished, "dest_slots": dest_slots}


EPSILON = 1e-06

def reference(prior_state, queries, new_keys, new_values, out_gates, decay_rates, norm_gain, out_weight, residual, ffn_gain, router_weight, gate_weight, up_weight, down_weight, expert_picks, finished, dest_slots):
    current = prior_state
    outputs = []
    for step_index in range(STEPS):
        keys_now = new_keys[step_index].astype(jnp.float32)
        values_now = new_values[step_index].astype(jnp.float32)
        query_now = queries[step_index].astype(jnp.float32)
        current = decay_rates[None, :, None, None] * current + keys_now[:, :, :, None] * values_now[:, :, None, :]
        attended = jnp.einsum('rhk,rhkv->rhv', query_now, current, precision=lax.Precision.HIGHEST)
        squares = lax.optimization_barrier(jnp.sum(attended * attended, axis=(1, 2)))
        gated_out = (attended * norm_gain[None] * jax.nn.sigmoid(out_gates[step_index].astype(jnp.float32))).astype(jnp.bfloat16)
        proj = jnp.einsum('rhv,hvd->rd', gated_out.astype(jnp.float32), out_weight.astype(jnp.float32))
        mixed_rows = residual[step_index].astype(jnp.float32) + proj * lax.rsqrt(squares / (HEADS * HEAD_DIM) + EPSILON)[:, None]
        normed = (mixed_rows * lax.rsqrt(lax.optimization_barrier(jnp.mean(mixed_rows * mixed_rows, axis=1, keepdims=True)) + EPSILON) * ffn_gain).astype(jnp.bfloat16)
        logits = jnp.dot(normed, router_weight, preferred_element_type=jnp.float32)
        picks_now = expert_picks[step_index]
        picked_logits = jnp.take_along_axis(logits, picks_now, axis=1)
        first_weight = jax.nn.sigmoid(picked_logits[:, 0] - picked_logits[:, 1])
        second_weight = jax.nn.sigmoid(picked_logits[:, 1] - picked_logits[:, 0])
        expert_ids = jnp.arange(EXPERTS, dtype=jnp.int32)
        weight_table = first_weight[:, None] * (picks_now[:, 0:1] == expert_ids[None, :]).astype(jnp.float32) + second_weight[:, None] * (picks_now[:, 1:2] == expert_ids[None, :]).astype(jnp.float32)

        def one_expert(expert_index):
            start = expert_index * FF
            gate_cols = lax.dynamic_slice_in_dim(gate_weight, start, FF, 1)
            up_cols = lax.dynamic_slice_in_dim(up_weight, start, FF, 1)
            down_rows = lax.dynamic_slice_in_dim(down_weight, start, FF, 0)
            gate_pre = jnp.dot(normed, gate_cols, preferred_element_type=jnp.float32)
            upward = jnp.dot(normed, up_cols, preferred_element_type=jnp.float32)
            hidden = (jax.nn.silu(gate_pre) * upward).astype(jnp.bfloat16)
            return jnp.dot(hidden, down_rows, preferred_element_type=jnp.float32)
        produced = lax.map(one_expert, expert_ids)
        moe_rows = jnp.einsum('re,erd->rd', weight_table, produced, precision=lax.Precision.HIGHEST)
        alive_rows = (1 - finished[step_index]).astype(jnp.float32)
        final_rows = ((mixed_rows + moe_rows) * alive_rows[:, None]).astype(jnp.bfloat16)
        placed = jnp.zeros((ROWS, D), jnp.bfloat16).at[dest_slots[step_index]].set(final_rows)
        outputs.append(placed)
    return jnp.stack(outputs, axis=0)
```

```python
import jax
import jax.numpy as jnp
from jax import lax
from jax.sharding import PartitionSpec as P

HEADS = 32
HEAD_DIM = 128
STEPS = 2


EPSILON = 1e-06


def local(
    prior_state,
    queries,
    new_keys,
    new_values,
    out_gates,
    decay_rates,
    norm_gain,
    out_weight,
    residual,
    ffn_gain,
    router_weight,
    gate_weight,
    up_weight,
    down_weight,
    expert_picks,
    finished,
    dest_slots,
):
    f32, bf16 = jnp.float32, jnp.bfloat16
    row_devices = lax.axis_size("row")
    shares = lax.axis_size(("head", "sub"))
    rows = queries.shape[1]
    experts = router_weight.shape[1]
    width = residual.shape[2]
    share_width = width // shares
    owners = row_devices // experts
    row_index = lax.axis_index("row")
    share_index = lax.axis_index(("head", "sub"))
    read = jnp.einsum(
        "srhk,rhkv->srhv", queries, prior_state.astype(bf16), preferred_element_type=f32
    )
    q, k, v = queries.astype(f32), new_keys.astype(f32), new_values.astype(f32)
    d = decay_rates[None, :, None]
    score = lambda s, t: jnp.sum(q[s] * k[t], axis=2, keepdims=True)
    first = d * read[0] + score(0, 0) * v[0]
    second = d * (d * read[1] + score(1, 0) * v[0]) + score(1, 1) * v[1]
    attended = jnp.stack([first, second])
    squares = jnp.sum(attended * attended, axis=(2, 3))
    gated = (attended * norm_gain * jax.nn.sigmoid(out_gates.astype(f32))).astype(bf16)
    partial = jnp.dot(
        gated.reshape(STEPS * rows, -1),
        out_weight.reshape(-1, width),
        preferred_element_type=f32,
    )
    proj, square_sum = lax.psum((partial, squares.reshape(STEPS * rows)), ("head", "sub"))
    mixed = (
        residual.reshape(STEPS * rows, width).astype(f32)
        + proj * lax.rsqrt(square_sum / (HEADS * HEAD_DIM) + EPSILON)[:, None]
    )
    normed = (
        mixed * lax.rsqrt(jnp.mean(mixed * mixed, axis=1, keepdims=True) + EPSILON) * ffn_gain
    ).astype(bf16)
    facts = jnp.concatenate(
        [expert_picks, finished[:, :, None], dest_slots[:, :, None]], axis=2
    ).reshape(STEPS * rows, 4)
    facts = lax.all_gather(facts, "row", axis=0, tiled=True)
    everyone = lax.all_gather(normed, "row", axis=0, tiled=True)
    logits = jnp.dot(everyone, router_weight, preferred_element_type=f32)
    expert_ids = lax.iota(jnp.int32, experts)[None, :]
    chosen_a = facts[:, 0:1] == expert_ids
    chosen_b = facts[:, 1:2] == expert_ids
    gap = jnp.sum(jnp.where(chosen_a, logits, 0.0), 1) - jnp.sum(jnp.where(chosen_b, logits, 0.0), 1)
    mine = row_index // owners
    share_of = jnp.where(facts[:, 0] == mine, jax.nn.sigmoid(gap), 0.0) + jnp.where(
        facts[:, 1] == mine, jax.nn.sigmoid(-gap), 0.0
    )
    share_of = share_of * (1 - facts[:, 2]).astype(f32)
    gate_pre = jnp.dot(everyone, gate_weight, preferred_element_type=f32)
    upward = jnp.dot(everyone, up_weight, preferred_element_type=f32)
    hidden = (jax.nn.silu(gate_pre) * upward * share_of[:, None]).astype(bf16)
    spots = lax.iota(jnp.int32, row_devices * STEPS * rows)
    spot_step = (spots // rows) % STEPS
    spot_slot = spots // (STEPS * rows) * rows + spots % rows
    mover = (spot_step[:, None] == spot_step[None, :]) & (spot_slot[:, None] == facts[None, :, 3])
    hidden = jnp.dot(mover.astype(bf16), hidden, preferred_element_type=f32).astype(bf16)
    produced = jnp.dot(hidden, down_weight, preferred_element_type=f32)
    own_step = lax.iota(jnp.int32, STEPS * rows) // rows
    own_mover = (spot_step[:, None] == own_step[None, :]) & (
        spot_slot[:, None] == dest_slots.reshape(-1)[None, :]
    )
    mixed_share = lax.dynamic_slice_in_dim(mixed, share_index * share_width, share_width, 1)
    mixed_share = mixed_share * (1 - finished).astype(f32).reshape(-1, 1)
    placed = jnp.dot(own_mover.astype(f32), mixed_share, precision=lax.Precision.HIGHEST)
    reduced = lax.psum_scatter(produced, ("head", "sub"), scatter_dimension=1, tiled=True)
    final = lax.psum_scatter(reduced + placed, "row", scatter_dimension=0, tiled=True)
    return final.astype(bf16).reshape(STEPS, rows, share_width)


def solution(mesh):
    in_specs = (
        P(("group", "row"), "head", None, "sub"),
        P(None, ("group", "row"), "head", None),
        P(None, ("group", "row"), "head", None),
        P(None, ("group", "row"), "head", "sub"),
        P(None, ("group", "row"), "head", "sub"),
        P("head"),
        P("head", "sub"),
        P("head", "sub", None),
        P(None, ("group", "row"), None),
        P(),
        P(),
        P(None, ("row", "head", "sub")),
        P(None, ("row", "head", "sub")),
        P(("row", "head", "sub"), None),
        P(None, ("group", "row"), None),
        P(None, ("group", "row")),
        P(None, ("group", "row")),
    )
    out_specs = P(None, ("group", "row"), ("head", "sub"))
    return jax.shard_map(local, mesh=mesh, in_specs=in_specs, out_specs=out_specs, check_vma=False)
```

```python
import functools

import jax
import jax.numpy as jnp
from jax import lax
from jax.experimental import pallas as pl
from jax.experimental.pallas import tpu as pltpu
from jax.sharding import PartitionSpec as P

HEADS = 32
HEAD_DIM = 128
STEPS = 2


EPSILON = 1e-06


def local(
    prior_state,
    queries,
    new_keys,
    new_values,
    out_gates,
    decay_rates,
    norm_gain,
    out_weight,
    residual,
    ffn_gain,
    router_weight,
    gate_weight,
    up_weight,
    down_weight,
    expert_picks,
    finished,
    dest_slots,
):
    f32, bf16 = jnp.float32, jnp.bfloat16
    row_devices = lax.axis_size("row")
    shares = lax.axis_size(("head", "sub"))
    rows = queries.shape[1]
    experts = router_weight.shape[1]
    width = residual.shape[2]
    share_width = width // shares
    owners = row_devices // experts
    row_index = lax.axis_index("row")
    share_index = lax.axis_index(("head", "sub"))
    read = jnp.einsum(
        "srhk,rhkv->srhv", queries, prior_state.astype(bf16), preferred_element_type=f32
    )
    q, k, v = queries.astype(f32), new_keys.astype(f32), new_values.astype(f32)
    d = decay_rates[None, :, None]
    score = lambda s, t: jnp.sum(q[s] * k[t], axis=2, keepdims=True)
    first = d * read[0] + score(0, 0) * v[0]
    second = d * (d * read[1] + score(1, 0) * v[0]) + score(1, 1) * v[1]
    attended = jnp.stack([first, second])
    squares = jnp.sum(attended * attended, axis=(2, 3))
    gated = (attended * norm_gain * jax.nn.sigmoid(out_gates.astype(f32))).astype(bf16)
    partial = jnp.dot(
        gated.reshape(STEPS * rows, -1),
        out_weight.reshape(-1, width),
        preferred_element_type=f32,
    )
    proj, square_sum = lax.psum((partial, squares.reshape(STEPS * rows)), ("head", "sub"))
    mixed = (
        residual.reshape(STEPS * rows, width).astype(f32)
        + proj * lax.rsqrt(square_sum / (HEADS * HEAD_DIM) + EPSILON)[:, None]
    )
    normed = (
        mixed * lax.rsqrt(jnp.mean(mixed * mixed, axis=1, keepdims=True) + EPSILON) * ffn_gain
    ).astype(bf16)
    facts = jnp.concatenate(
        [expert_picks, finished[:, :, None], dest_slots[:, :, None]], axis=2
    ).reshape(STEPS * rows, 4)
    facts = lax.all_gather(facts, "row", axis=0, tiled=True)
    everyone = lax.all_gather(normed, "row", axis=0, tiled=True)
    logits = jnp.dot(everyone, router_weight, preferred_element_type=f32)
    expert_ids = lax.iota(jnp.int32, experts)[None, :]
    chosen_a = facts[:, 0:1] == expert_ids
    chosen_b = facts[:, 1:2] == expert_ids
    gap = jnp.sum(jnp.where(chosen_a, logits, 0.0), 1) - jnp.sum(jnp.where(chosen_b, logits, 0.0), 1)
    mine = row_index // owners
    share_of = jnp.where(facts[:, 0] == mine, jax.nn.sigmoid(gap), 0.0) + jnp.where(
        facts[:, 1] == mine, jax.nn.sigmoid(-gap), 0.0
    )
    share_of = share_of * (1 - facts[:, 2]).astype(f32)
    gate_pre = jnp.dot(everyone, gate_weight, preferred_element_type=f32)
    upward = jnp.dot(everyone, up_weight, preferred_element_type=f32)
    hidden = (jax.nn.silu(gate_pre) * upward * share_of[:, None]).astype(bf16)
    spots = lax.iota(jnp.int32, row_devices * STEPS * rows)
    spot_step = (spots // rows) % STEPS
    spot_slot = spots // (STEPS * rows) * rows + spots % rows
    mover = (spot_step[:, None] == spot_step[None, :]) & (spot_slot[:, None] == facts[None, :, 3])
    hidden = jnp.dot(mover.astype(bf16), hidden, preferred_element_type=f32).astype(bf16)
    produced = jnp.dot(hidden, down_weight, preferred_element_type=f32)
    own_step = lax.iota(jnp.int32, STEPS * rows) // rows
    own_mover = (spot_step[:, None] == own_step[None, :]) & (
        spot_slot[:, None] == dest_slots.reshape(-1)[None, :]
    )
    mixed_share = lax.dynamic_slice_in_dim(mixed, share_index * share_width, share_width, 1)
    mixed_share = mixed_share * (1 - finished).astype(f32).reshape(-1, 1)
    placed = jnp.dot(own_mover.astype(f32), mixed_share, precision=lax.Precision.HIGHEST)
    reduced = lax.psum_scatter(produced, ("head", "sub"), scatter_dimension=1, tiled=True)
    final = lax.psum_scatter(reduced + placed, "row", scatter_dimension=0, tiled=True)
    return final.astype(bf16).reshape(STEPS, rows, share_width)


def high_low(value, lanes):
    high = value.astype(jnp.bfloat16).astype(jnp.float32)
    return jnp.where(lanes < 64, high, value - high)


def column_of(ext):
    return ext[:, 0:1].astype(jnp.float32) + ext[:, 64:65].astype(jnp.float32)


def fused_kernel(
    n,
    experts,
    decay_s,
    q_h, k_h, v_h, g_h, gain_h, res_h, fgain_h, router_h, meta_h,
    state_h, wo_h, wg_h, wu_h, wd_h,
    out_ref,
    q_b, k_b, v_b, g_b, gain_b, res_b, fgain_b, router_b,
    state_b, wo_b, wg_b, wu_b, wd_b,
    q32, k32, v32, g32, gated_b, facts_b, mix_b,
    a_send, a_recv, x_all, acc_g, acc_u, hid_b, d_send, d_recv, y_b, y_send, y_recv,
    small_sem, state_sem, wo_sem, wg_sem, wu_sem, wd_sem,
    facts_ss, facts_rs, a_ss, a_rs, z_ss, z_rs, x_ss, x_rs, s_ss, s_rs, f_ss, f_rs,
    d_ss, d_rs, y_ss, y_rs,
):
    f32, bf16 = jnp.float32, jnp.bfloat16
    z, x, c = lax.axis_index("row"), lax.axis_index("head"), lax.axis_index("sub")
    tokens, share = out_ref.shape
    rows = tokens // STEPS
    heads, wide = gain_b.shape
    hidden_width = wg_b.shape[2]
    width = 4 * share
    own, sib = 2 * x + c, 2 * x + 1 - c
    far, cross = 2 * (1 - x) + c, 2 * (1 - x) + 1 - c
    sibling, opposite = {"sub": 1 - c}, {"head": 1 - x}
    mesh_id = pl.DeviceIdType.MESH

    def part(index):
        return pl.ds(pl.multiple_of(index * share, 128), share)

    def row_part(index):
        return pl.ds(pl.multiple_of(index * tokens, 16), tokens)

    def remote(src, dst, ss, rs, where):
        return pltpu.make_async_remote_copy(
            src_ref=src, dst_ref=dst, send_sem=ss, recv_sem=rs,
            device_id=where, device_id_type=mesh_id,
        )

    smalls = [
        (q_h, q_b), (k_h, k_b), (v_h, v_b), (g_h, g_b), (gain_h, gain_b),
        (res_h.at[:, part(own)], res_b), (fgain_h.at[:, part(own)], fgain_b),
        (router_h, router_b), (meta_h, facts_b.at[row_part(z), :]),
    ]
    small_copies = [
        pltpu.make_async_copy(a, b, small_sem.at[i]) for i, (a, b) in enumerate(smalls)
    ]
    state_copy = pltpu.make_async_copy(state_h, state_b, state_sem.at[0])
    out_order = (cross, sib, far, own)
    in_order = (own, sib, far, cross)
    wo_copies = [
        pltpu.make_async_copy(wo_h.at[:, part(j)], wo_b.at[i], wo_sem.at[i])
        for i, j in enumerate(out_order)
    ]
    wg_copies = [
        pltpu.make_async_copy(wg_h.at[part(j), :], wg_b.at[i], wg_sem.at[i])
        for i, j in enumerate(in_order)
    ]
    wu_copies = [
        pltpu.make_async_copy(wu_h.at[part(j), :], wu_b.at[i], wu_sem.at[i])
        for i, j in enumerate(in_order)
    ]
    wd_copies = [
        pltpu.make_async_copy(wd_h.at[:, part(j)], wd_b.at[i], wd_sem.at[i])
        for i, j in enumerate(out_order)
    ]
    for copy in small_copies:
        copy.start()
    state_copy.start()
    for copy in wo_copies:
        copy.start()
    for i in range(4):
        wg_copies[i].start()
        wu_copies[i].start()
    for copy in wd_copies:
        copy.start()

    barrier = pltpu.get_barrier_semaphore()
    peers = [{"row": lax.rem(z + d, n)} for d in range(1, n)] + [sibling, opposite]
    for peer in peers:
        pl.semaphore_signal(barrier, inc=1, device_id=peer, device_id_type=mesh_id)

    for copy in small_copies:
        copy.wait()
    q32[...] = q_b[...].astype(f32)
    k32[...] = k_b[...].astype(f32)
    v32[...] = v_b[...].astype(f32)
    g32[...] = g_b[...].astype(f32)
    state_copy.wait()
    row_ids = lax.broadcasted_iota(jnp.int32, (tokens, 128), 0) % rows
    squares = jnp.zeros((tokens, wide), f32)
    pending = None
    for h in range(heads):
        picked = pl.ds(h, tokens, stride=heads)
        q, k, v, g = q32[picked, :], k32[picked, :], v32[picked, :], g32[picked, :]
        table = state_b[:, h, :, :].astype(bf16).reshape(rows * wide, state_b.shape[3])
        read = lax.dot_general(
            q.astype(bf16), table, (((1,), (1,)), ((), ())), preferred_element_type=f32
        )
        pairs = jnp.zeros((tokens, 2 * wide), f32)
        for p in range(rows // 2):
            pairs = jnp.where(row_ids // 2 == p, read[:, p * 128 : (p + 1) * 128], pairs)
        kept = jnp.where(row_ids[:, :wide] % 2 == 0, pairs[:, :wide], pairs[:, wide:])
        d = decay_s[0, h]
        one = lambda s, t: jnp.sum(
            q[s * rows : (s + 1) * rows] * k[t * rows : (t + 1) * rows], axis=1, keepdims=True
        )
        v0, v1 = v[:rows], v[rows:]
        first = d * kept[:rows] + one(0, 0) * v0
        second = d * (d * kept[rows:] + one(1, 0) * v0) + one(1, 1) * v1
        attended = jnp.concatenate([first, second], axis=0)
        squares = squares + attended * attended
        gated = attended * gain_b[h : h + 1, :] * jax.nn.sigmoid(g)
        if h % 2 == 0:
            pending = gated
        else:
            both = jnp.concatenate([pending, gated], axis=1)
            gated_b[:, (h // 2) * 128 : (h // 2 + 1) * 128] = both.astype(bf16)
    square_part = jnp.sum(squares, axis=1, keepdims=True)
    lanes = lax.broadcasted_iota(jnp.int32, (tokens, 128), 1)

    pl.semaphore_wait(barrier, n + 1)
    facts_copies = []
    for d in range(1, n):
        copy = remote(
            facts_b.at[row_part(z), :], facts_b.at[row_part(z), :],
            facts_ss.at[d - 1], facts_rs.at[d - 1], {"row": lax.rem(z + d, n)},
        )
        copy.start()
        facts_copies.append(copy)

    def project(i):
        wo_copies[i].wait()
        return jnp.dot(gated_b[...], wo_b[i], preferred_element_type=f32)

    def a_pack(slot, value, column):
        a_send[slot, :, :share] = value.astype(bf16)
        a_send[slot, :, share:] = high_low(column, lanes).astype(bf16)

    a_copies = [
        remote(a_send.at[i], a_recv.at[i], a_ss.at[i], a_rs.at[i], where)
        for i, where in enumerate((sibling, sibling, opposite))
    ]
    for i in range(2):
        a_pack(i, project(i), square_part)
        a_copies[i].start()
    value = project(2)
    a_copies[0].wait_recv()
    a_pack(
        2, value + a_recv[0, :, :share].astype(f32), square_part + column_of(a_recv[0, :, share:])
    )
    a_copies[2].start()
    value = project(3)
    a_copies[1].wait_recv()
    value = value + a_recv[1, :, :share].astype(f32)
    a_copies[2].wait_recv()
    value = value + a_recv[2, :, :share].astype(f32)
    total_square = (
        square_part + column_of(a_recv[1, :, share:]) + column_of(a_recv[2, :, share:])
    )
    mixed = res_b[...].astype(f32) + value * lax.rsqrt(
        total_square / (HEADS * HEAD_DIM) + EPSILON
    )
    mix_b[...] = mixed
    mixed_square = jnp.sum(mixed * mixed, axis=1, keepdims=True)
    x_all[own, row_part(z), :share] = (mixed * fgain_b[...]).astype(bf16)
    x_all[own, row_part(z), share:] = high_low(mixed_square, lanes).astype(bf16)

    def block(j, d):
        return x_all.at[j, row_part(lax.rem(z - d + n, n)), :]

    z_copies = [
        remote(block(own, 0), block(own, 0), z_ss.at[d - 1], z_rs.at[d - 1],
               {"row": lax.rem(z + d, n)})
        for d in range(1, n)
    ]
    x_copies = [
        remote(block(own, d), block(own, d), x_ss.at[d], x_rs.at[d], opposite) for d in range(n)
    ]
    s_copies = [
        remote(block(own, d), block(own, d), s_ss.at[d], s_rs.at[d], sibling) for d in range(n)
    ]
    f_copies = [
        remote(block(far, d), block(far, d), f_ss.at[d], f_rs.at[d], sibling) for d in range(n)
    ]
    for copy in z_copies:
        copy.start()
    x_copies[0].start()
    s_copies[0].start()
    for d in range(1, n):
        z_copies[d - 1].wait_recv()
        x_copies[d].start()
        s_copies[d].start()

    chunk = 512
    scores = [jnp.zeros((n * tokens, 1), f32) for _ in range(experts)]
    mean_sum = jnp.zeros((n * tokens, 1), f32)
    for i, j in enumerate(in_order):
        if i == 1:
            for d in range(n):
                x_copies[d].wait_recv()
                f_copies[d].start()
            for d in range(n):
                s_copies[d].wait_recv()
        if i == 3:
            for d in range(n):
                f_copies[d].wait_recv()
        wg_copies[i].wait()
        wu_copies[i].wait()
        left = x_all[j, :, :share]
        for m in range(hidden_width // chunk):
            columns = pl.ds(m * chunk, chunk)
            gate_term = jnp.dot(left, wg_b[i, :, columns], preferred_element_type=f32)
            up_term = jnp.dot(left, wu_b[i, :, columns], preferred_element_type=f32)
            if i == 0:
                acc_g[:, columns] = gate_term
                acc_u[:, columns] = up_term
            else:
                acc_g[:, columns] += gate_term
                acc_u[:, columns] += up_term
        wide_left = left.astype(f32)
        mean_sum = mean_sum + column_of(x_all[j, :, share:])
        for e in range(experts):
            weights = router_b[e : e + 1, part(j)].astype(f32)
            scores[e] = scores[e] + jnp.sum(wide_left * weights, axis=1, keepdims=True)

    for copy in facts_copies:
        copy.wait_recv()
    facts = facts_b[...]
    scale = lax.rsqrt(mean_sum / width + EPSILON)
    pick_a, pick_b = facts[:, 0:1], facts[:, 1:2]
    gap = jnp.zeros_like(scale)
    for e in range(experts):
        gap = gap + jnp.where(pick_a == e, scores[e], 0.0) - jnp.where(pick_b == e, scores[e], 0.0)
    gap = gap * scale
    mine = (z // (n // experts)).astype(f32)
    share_of = jnp.where(pick_a == mine, jax.nn.sigmoid(gap), 0.0) + jnp.where(
        pick_b == mine, jax.nn.sigmoid(-gap), 0.0
    )
    share_of = share_of * (1.0 - facts[:, 2:3])

    def mover_of(entries, first_step_rows):
        count = entries.shape[0]
        field = lax.broadcasted_iota(jnp.int32, (n * tokens, 128), 1)
        picker = jnp.where(field == 3, 1.0, 0.0).astype(bf16)
        slots = lax.dot_general(
            picker, entries.astype(bf16), (((1,), (1,)), ((), ())), preferred_element_type=f32
        )
        place = lax.broadcasted_iota(jnp.int32, (n * tokens, count), 0)
        source = lax.broadcasted_iota(jnp.int32, (n * tokens, count), 1)
        same = (place // rows) % STEPS == (source // rows) % STEPS
        slot = (place // tokens * rows + place % rows).astype(f32)
        return jnp.where(same & (slots == slot), 1.0, 0.0).astype(bf16)

    mover = mover_of(facts, None)
    for m in range(hidden_width // chunk):
        columns = pl.ds(m * chunk, chunk)
        gate_pre = acc_g[:, columns] * scale
        upward = acc_u[:, columns] * scale
        hidden = (gate_pre * jax.nn.sigmoid(gate_pre) * upward * share_of).astype(bf16)
        hid_b[:, columns] = jnp.dot(mover, hidden, preferred_element_type=f32).astype(bf16)

    def lower(i, y):
        wd_copies[i].wait()
        return jnp.dot(hid_b[...], wd_b[i], preferred_element_type=f32)

    d_copies = [
        remote(d_send.at[i], d_recv.at[i], d_ss.at[i], d_rs.at[i], where)
        for i, where in enumerate((sibling, sibling, opposite))
    ]
    for i in range(2):
        d_send[i] = lower(i, None).astype(bf16)
        d_copies[i].start()
    value = lower(2, None)
    d_copies[0].wait_recv()
    d_send[2] = (value + d_recv[0].astype(f32)).astype(bf16)
    d_copies[2].start()
    value = lower(3, None)
    own_facts = facts_b[row_part(z), :]
    own_mover = mover_of(own_facts, None)
    kept_mix = mix_b[...] * (1.0 - own_facts[:, 2:3])
    mix_high = kept_mix.astype(bf16)
    mix_low = (kept_mix - mix_high.astype(f32)).astype(bf16)
    value = value + jnp.dot(own_mover, mix_high, preferred_element_type=f32)
    value = value + jnp.dot(own_mover, mix_low, preferred_element_type=f32)
    d_copies[1].wait_recv()
    value = value + d_recv[1].astype(f32)
    d_copies[2].wait_recv()
    value = value + d_recv[2].astype(f32)
    y_b[...] = value
    y_send[...] = value.astype(bf16)
    y_copies = []
    for d in range(1, n):
        there = lax.rem(z + d, n)
        copy = remote(
            y_send.at[row_part(there), :], y_recv.at[d - 1], y_ss.at[d - 1], y_rs.at[d - 1],
            {"row": there},
        )
        copy.start()
        y_copies.append(copy)
    total = y_b[row_part(z), :]
    for d in range(1, n):
        y_copies[d - 1].wait_recv()
        total = total + y_recv[d - 1].astype(f32)
    out_ref[...] = total.astype(bf16)
    for copy in (
        facts_copies + a_copies + z_copies + x_copies + s_copies + f_copies + d_copies + y_copies
    ):
        copy.wait_send()


def fused_local(
    prior_state,
    queries,
    new_keys,
    new_values,
    out_gates,
    decay_rates,
    norm_gain,
    out_weight,
    residual,
    ffn_gain,
    router_weight,
    gate_weight,
    up_weight,
    down_weight,
    expert_picks,
    finished,
    dest_slots,
):
    f32, bf16 = jnp.float32, jnp.bfloat16
    n = lax.axis_size("row")
    rows, heads, key_dim = queries.shape[1:]
    wide = new_values.shape[3]
    width = residual.shape[2]
    share = width // 4
    experts = router_weight.shape[1]
    hidden = gate_weight.shape[1]
    tokens = STEPS * rows
    flat = tokens * heads
    facts = jnp.concatenate(
        [expert_picks, finished[:, :, None], dest_slots[:, :, None]], axis=2
    ).reshape(tokens, 4)
    facts = jnp.pad(facts.astype(f32), ((0, 0), (0, 124)))
    any_space = pl.BlockSpec(memory_space=pl.ANY)
    dma = pltpu.SemaphoreType.DMA
    out = pl.pallas_call(
        functools.partial(fused_kernel, n, experts),
        out_shape=jax.ShapeDtypeStruct((tokens, share), bf16),
        in_specs=[pl.BlockSpec(memory_space=pltpu.SMEM)] + [any_space] * 14,
        out_specs=pl.BlockSpec(memory_space=pltpu.VMEM),
        scratch_shapes=[
            pltpu.VMEM((flat, key_dim), bf16),
            pltpu.VMEM((flat, key_dim), bf16),
            pltpu.VMEM((flat, wide), bf16),
            pltpu.VMEM((flat, wide), bf16),
            pltpu.VMEM((heads, wide), f32),
            pltpu.VMEM((tokens, share), bf16),
            pltpu.VMEM((1, share), f32),
            pltpu.VMEM((experts, width), bf16),
            pltpu.VMEM((rows, heads, wide, key_dim), f32),
            pltpu.VMEM((4, heads * wide, share), bf16),
            pltpu.VMEM((4, share, hidden), bf16),
            pltpu.VMEM((4, share, hidden), bf16),
            pltpu.VMEM((4, hidden, share), bf16),
            pltpu.VMEM((flat, key_dim), f32),
            pltpu.VMEM((flat, key_dim), f32),
            pltpu.VMEM((flat, wide), f32),
            pltpu.VMEM((flat, wide), f32),
            pltpu.VMEM((tokens, heads * wide), bf16),
            pltpu.VMEM((n * tokens, 128), f32),
            pltpu.VMEM((tokens, share), f32),
            pltpu.VMEM((3, tokens, share + 128), bf16),
            pltpu.VMEM((3, tokens, share + 128), bf16),
            pltpu.VMEM((4, n * tokens, share + 128), bf16),
            pltpu.VMEM((n * tokens, hidden), f32),
            pltpu.VMEM((n * tokens, hidden), f32),
            pltpu.VMEM((n * tokens, hidden), bf16),
            pltpu.VMEM((3, n * tokens, share), bf16),
            pltpu.VMEM((3, n * tokens, share), bf16),
            pltpu.VMEM((n * tokens, share), f32),
            pltpu.VMEM((n * tokens, share), bf16),
            pltpu.VMEM((n - 1, tokens, share), bf16),
            dma((9,)), dma((1,)), dma((4,)), dma((4,)), dma((4,)), dma((4,)),
            dma((n - 1,)), dma((n - 1,)), dma((3,)), dma((3,)), dma((n - 1,)), dma((n - 1,)),
            dma((n,)), dma((n,)), dma((n,)), dma((n,)), dma((n,)), dma((n,)),
            dma((3,)), dma((3,)), dma((n - 1,)), dma((n - 1,)),
        ],
        compiler_params=pltpu.CompilerParams(
            collective_id=0, has_side_effects=True, vmem_limit_bytes=58 * 1024 * 1024
        ),
    )(
        decay_rates.reshape(1, heads),
        queries.reshape(flat, key_dim),
        new_keys.reshape(flat, key_dim),
        new_values.reshape(flat, wide),
        out_gates.reshape(flat, wide),
        norm_gain,
        residual.reshape(tokens, width),
        ffn_gain.reshape(1, width),
        router_weight.T,
        facts,
        jnp.swapaxes(prior_state, 2, 3),
        out_weight.reshape(heads * wide, width),
        gate_weight,
        up_weight,
        down_weight,
    )
    return out.reshape(STEPS, rows, share)


def solution(mesh):
    in_specs = (
        P(("group", "row"), "head", None, "sub"),
        P(None, ("group", "row"), "head", None),
        P(None, ("group", "row"), "head", None),
        P(None, ("group", "row"), "head", "sub"),
        P(None, ("group", "row"), "head", "sub"),
        P("head"),
        P("head", "sub"),
        P("head", "sub", None),
        P(None, ("group", "row"), None),
        P(),
        P(),
        P(None, ("row", "head", "sub")),
        P(None, ("row", "head", "sub")),
        P(("row", "head", "sub"), None),
        P(None, ("group", "row"), None),
        P(None, ("group", "row")),
        P(None, ("group", "row")),
    )
    out_specs = P(None, ("group", "row"), ("head", "sub"))
    small = mesh.shape["head"] == 2 and mesh.shape["sub"] == 2 and mesh.shape["row"] in (4, 8)
    part_program = fused_local if small else local
    return jax.shard_map(part_program, mesh=mesh, in_specs=in_specs, out_specs=out_specs, check_vma=False)
```

```python
import functools

import jax
import jax.numpy as jnp
from jax import lax
from jax.experimental import pallas as pl
from jax.experimental.pallas import tpu as pltpu
from jax.sharding import PartitionSpec as P

HEADS = 32
HEAD_DIM = 128
STEPS = 2


EPSILON = 1e-06


def local(
    prior_state,
    queries,
    new_keys,
    new_values,
    out_gates,
    decay_rates,
    norm_gain,
    out_weight,
    residual,
    ffn_gain,
    router_weight,
    gate_weight,
    up_weight,
    down_weight,
    expert_picks,
    finished,
    dest_slots,
):
    f32, bf16 = jnp.float32, jnp.bfloat16
    row_devices = lax.axis_size("row")
    shares = lax.axis_size(("head", "sub"))
    rows = queries.shape[1]
    experts = router_weight.shape[1]
    width = residual.shape[2]
    share_width = width // shares
    owners = row_devices // experts
    row_index = lax.axis_index("row")
    share_index = lax.axis_index(("head", "sub"))
    read = jnp.einsum(
        "srhk,rhkv->srhv", queries, prior_state.astype(bf16), preferred_element_type=f32
    )
    q, k, v = queries.astype(f32), new_keys.astype(f32), new_values.astype(f32)
    d = decay_rates[None, :, None]
    score = lambda s, t: jnp.sum(q[s] * k[t], axis=2, keepdims=True)
    first = d * read[0] + score(0, 0) * v[0]
    second = d * (d * read[1] + score(1, 0) * v[0]) + score(1, 1) * v[1]
    attended = jnp.stack([first, second])
    squares = jnp.sum(attended * attended, axis=(2, 3))
    gated = (attended * norm_gain * jax.nn.sigmoid(out_gates.astype(f32))).astype(bf16)
    partial = jnp.dot(
        gated.reshape(STEPS * rows, -1),
        out_weight.reshape(-1, width),
        preferred_element_type=f32,
    )
    proj, square_sum = lax.psum((partial, squares.reshape(STEPS * rows)), ("head", "sub"))
    mixed = (
        residual.reshape(STEPS * rows, width).astype(f32)
        + proj * lax.rsqrt(square_sum / (HEADS * HEAD_DIM) + EPSILON)[:, None]
    )
    normed = (
        mixed * lax.rsqrt(jnp.mean(mixed * mixed, axis=1, keepdims=True) + EPSILON) * ffn_gain
    ).astype(bf16)
    facts = jnp.concatenate(
        [expert_picks, finished[:, :, None], dest_slots[:, :, None]], axis=2
    ).reshape(STEPS * rows, 4)
    facts = lax.all_gather(facts, "row", axis=0, tiled=True)
    everyone = lax.all_gather(normed, "row", axis=0, tiled=True)
    logits = jnp.dot(everyone, router_weight, preferred_element_type=f32)
    expert_ids = lax.iota(jnp.int32, experts)[None, :]
    chosen_a = facts[:, 0:1] == expert_ids
    chosen_b = facts[:, 1:2] == expert_ids
    gap = jnp.sum(jnp.where(chosen_a, logits, 0.0), 1) - jnp.sum(jnp.where(chosen_b, logits, 0.0), 1)
    mine = row_index // owners
    share_of = jnp.where(facts[:, 0] == mine, jax.nn.sigmoid(gap), 0.0) + jnp.where(
        facts[:, 1] == mine, jax.nn.sigmoid(-gap), 0.0
    )
    share_of = share_of * (1 - facts[:, 2]).astype(f32)
    gate_pre = jnp.dot(everyone, gate_weight, preferred_element_type=f32)
    upward = jnp.dot(everyone, up_weight, preferred_element_type=f32)
    hidden = (jax.nn.silu(gate_pre) * upward * share_of[:, None]).astype(bf16)
    spots = lax.iota(jnp.int32, row_devices * STEPS * rows)
    spot_step = (spots // rows) % STEPS
    spot_slot = spots // (STEPS * rows) * rows + spots % rows
    mover = (spot_step[:, None] == spot_step[None, :]) & (spot_slot[:, None] == facts[None, :, 3])
    hidden = jnp.dot(mover.astype(bf16), hidden, preferred_element_type=f32).astype(bf16)
    produced = jnp.dot(hidden, down_weight, preferred_element_type=f32)
    own_step = lax.iota(jnp.int32, STEPS * rows) // rows
    own_mover = (spot_step[:, None] == own_step[None, :]) & (
        spot_slot[:, None] == dest_slots.reshape(-1)[None, :]
    )
    mixed_share = lax.dynamic_slice_in_dim(mixed, share_index * share_width, share_width, 1)
    mixed_share = mixed_share * (1 - finished).astype(f32).reshape(-1, 1)
    placed = jnp.dot(own_mover.astype(f32), mixed_share, precision=lax.Precision.HIGHEST)
    reduced = lax.psum_scatter(produced, ("head", "sub"), scatter_dimension=1, tiled=True)
    final = lax.psum_scatter(reduced + placed, "row", scatter_dimension=0, tiled=True)
    return final.astype(bf16).reshape(STEPS, rows, share_width)


def high_low(value, lanes):
    high = value.astype(jnp.bfloat16).astype(jnp.float32)
    return jnp.where(lanes < 64, high, value - high)


def column_of(ext):
    return ext[:, 0:1].astype(jnp.float32) + ext[:, 64:65].astype(jnp.float32)


def fused_kernel(
    n,
    experts,
    decay_s,
    q_h, k_h, v_h, g_h, gain_h, res_h, fgain_h, router_h, meta_h,
    state_h, wo_h, wg_h, wu_h, wd_h,
    out_ref,
    q_b, k_b, v_b, g_b, gain_b, res_b, fgain_b, router_b,
    state_b, wo_b, wg_b, wu_b, wd_b,
    q32, k32, v32, g32, gated_b, facts_b, mix_b,
    a_send, a_recv, x_all, acc_g, acc_u, hid_b, d_send, d_recv, y_b, y_send, y_recv,
    small_sem, state_sem, wo_sem, wg_sem, wu_sem, wd_sem,
    facts_ss, facts_rs, a_ss, a_rs, z_ss, z_rs, x_ss, x_rs, s_ss, s_rs, f_ss, f_rs,
    d_ss, d_rs, y_ss, y_rs,
):
    f32, bf16 = jnp.float32, jnp.bfloat16
    z, x, c = lax.axis_index("row"), lax.axis_index("head"), lax.axis_index("sub")
    tokens, share = out_ref.shape
    rows = tokens // STEPS
    heads, wide = gain_b.shape
    hidden_width = wg_b.shape[2]
    width = 4 * share
    own, sib = 2 * x + c, 2 * x + 1 - c
    far, cross = 2 * (1 - x) + c, 2 * (1 - x) + 1 - c
    sibling, opposite = {"sub": 1 - c}, {"head": 1 - x}
    mesh_id = pl.DeviceIdType.MESH

    def part(index):
        return pl.ds(pl.multiple_of(index * share, 128), share)

    def row_part(index):
        return pl.ds(pl.multiple_of(index * tokens, 16), tokens)

    def remote(src, dst, ss, rs, where):
        return pltpu.make_async_remote_copy(
            src_ref=src, dst_ref=dst, send_sem=ss, recv_sem=rs,
            device_id=where, device_id_type=mesh_id,
        )

    smalls = [
        (q_h, q_b), (k_h, k_b), (v_h, v_b), (g_h, g_b), (gain_h, gain_b),
        (res_h.at[:, part(own)], res_b), (fgain_h.at[:, part(own)], fgain_b),
        (router_h, router_b), (meta_h, facts_b.at[row_part(z), :]),
    ]
    small_copies = [
        pltpu.make_async_copy(a, b, small_sem.at[i]) for i, (a, b) in enumerate(smalls)
    ]
    state_copy = pltpu.make_async_copy(state_h, state_b, state_sem.at[0])
    out_order = (cross, sib, far, own)
    in_order = (own, sib, far, cross)
    wo_copies = [
        pltpu.make_async_copy(wo_h.at[:, part(j)], wo_b.at[i], wo_sem.at[i])
        for i, j in enumerate(out_order)
    ]
    wg_copies = [
        pltpu.make_async_copy(wg_h.at[part(j), :], wg_b.at[i], wg_sem.at[i])
        for i, j in enumerate(in_order)
    ]
    wu_copies = [
        pltpu.make_async_copy(wu_h.at[part(j), :], wu_b.at[i], wu_sem.at[i])
        for i, j in enumerate(in_order)
    ]
    wd_copies = [
        pltpu.make_async_copy(wd_h.at[:, part(j)], wd_b.at[i], wd_sem.at[i])
        for i, j in enumerate(out_order)
    ]
    for copy in small_copies:
        copy.start()
    state_copy.start()
    for copy in wo_copies:
        copy.start()

    barrier = pltpu.get_barrier_semaphore()
    peers = [{"row": lax.rem(z + d, n)} for d in range(1, n)] + [sibling, opposite]
    for peer in peers:
        pl.semaphore_signal(barrier, inc=1, device_id=peer, device_id_type=mesh_id)

    for copy in small_copies:
        copy.wait()
    q32[...] = q_b[...].astype(f32)
    k32[...] = k_b[...].astype(f32)
    v32[...] = v_b[...].astype(f32)
    g32[...] = g_b[...].astype(f32)
    state_copy.wait()
    for i in range(4):
        wg_copies[i].start()
        wu_copies[i].start()
    row_ids = lax.broadcasted_iota(jnp.int32, (tokens, 128), 0) % rows
    squares = jnp.zeros((tokens, wide), f32)
    pending = None
    for h in range(heads):
        picked = pl.ds(h, tokens, stride=heads)
        q, k, v, g = q32[picked, :], k32[picked, :], v32[picked, :], g32[picked, :]
        table = state_b[:, h, :, :].astype(bf16).reshape(rows * wide, state_b.shape[3])
        read = lax.dot_general(
            q.astype(bf16), table, (((1,), (1,)), ((), ())), preferred_element_type=f32
        )
        pairs = jnp.zeros((tokens, 2 * wide), f32)
        for p in range(rows // 2):
            pairs = jnp.where(row_ids // 2 == p, read[:, p * 128 : (p + 1) * 128], pairs)
        kept = jnp.where(row_ids[:, :wide] % 2 == 0, pairs[:, :wide], pairs[:, wide:])
        d = decay_s[0, h]
        one = lambda s, t: jnp.sum(
            q[s * rows : (s + 1) * rows] * k[t * rows : (t + 1) * rows], axis=1, keepdims=True
        )
        v0, v1 = v[:rows], v[rows:]
        first = d * kept[:rows] + one(0, 0) * v0
        second = d * (d * kept[rows:] + one(1, 0) * v0) + one(1, 1) * v1
        attended = jnp.concatenate([first, second], axis=0)
        squares = squares + attended * attended
        gated = attended * gain_b[h : h + 1, :] * jax.nn.sigmoid(g)
        if h % 2 == 0:
            pending = gated
        else:
            both = jnp.concatenate([pending, gated], axis=1)
            gated_b[:, (h // 2) * 128 : (h // 2 + 1) * 128] = both.astype(bf16)
    square_part = jnp.sum(squares, axis=1, keepdims=True)
    lanes = lax.broadcasted_iota(jnp.int32, (tokens, 128), 1)

    pl.semaphore_wait(barrier, n + 1)
    facts_copies = []
    for d in range(1, n):
        copy = remote(
            facts_b.at[row_part(z), :], facts_b.at[row_part(z), :],
            facts_ss.at[d - 1], facts_rs.at[d - 1], {"row": lax.rem(z + d, n)},
        )
        copy.start()
        facts_copies.append(copy)

    def project(i):
        wo_copies[i].wait()
        return jnp.dot(gated_b[...], wo_b[i], preferred_element_type=f32)

    def a_pack(slot, value, column):
        a_send[slot, :, :share] = value.astype(bf16)
        a_send[slot, :, share:] = high_low(column, lanes).astype(bf16)

    a_copies = [
        remote(a_send.at[i], a_recv.at[i], a_ss.at[i], a_rs.at[i], where)
        for i, where in enumerate((sibling, sibling, opposite))
    ]
    for i in range(2):
        a_pack(i, project(i), square_part)
        a_copies[i].start()
    value = project(2)
    a_copies[0].wait_recv()
    a_pack(
        2, value + a_recv[0, :, :share].astype(f32), square_part + column_of(a_recv[0, :, share:])
    )
    a_copies[2].start()
    value = project(3)
    a_copies[1].wait_recv()
    value = value + a_recv[1, :, :share].astype(f32)
    a_copies[2].wait_recv()
    value = value + a_recv[2, :, :share].astype(f32)
    total_square = (
        square_part + column_of(a_recv[1, :, share:]) + column_of(a_recv[2, :, share:])
    )
    mixed = res_b[...].astype(f32) + value * lax.rsqrt(
        total_square / (HEADS * HEAD_DIM) + EPSILON
    )
    mix_b[...] = mixed
    mixed_square = jnp.sum(mixed * mixed, axis=1, keepdims=True)
    x_all[own, row_part(z), :share] = (mixed * fgain_b[...]).astype(bf16)
    x_all[own, row_part(z), share:] = high_low(mixed_square, lanes).astype(bf16)

    def block(j, d):
        return x_all.at[j, row_part(lax.rem(z - d + n, n)), :]

    z_copies = [
        remote(block(own, 0), block(own, 0), z_ss.at[d - 1], z_rs.at[d - 1],
               {"row": lax.rem(z + d, n)})
        for d in range(1, n)
    ]
    x_copies = [
        remote(block(own, d), block(own, d), x_ss.at[d], x_rs.at[d], opposite) for d in range(n)
    ]
    s_copies = [
        remote(block(own, d), block(own, d), s_ss.at[d], s_rs.at[d], sibling) for d in range(n)
    ]
    f_copies = [
        remote(block(far, d), block(far, d), f_ss.at[d], f_rs.at[d], sibling) for d in range(n)
    ]
    for copy in z_copies:
        copy.start()
    x_copies[0].start()
    s_copies[0].start()
    for d in range(1, n):
        z_copies[d - 1].wait_recv()
        x_copies[d].start()
        s_copies[d].start()

    chunk = 512
    for copy in wd_copies:
        copy.start()
    scores = [jnp.zeros((n * tokens, 1), f32) for _ in range(experts)]
    mean_sum = jnp.zeros((n * tokens, 1), f32)
    for i, j in enumerate(in_order):
        if i == 1:
            for d in range(n):
                x_copies[d].wait_recv()
                f_copies[d].start()
            for d in range(n):
                s_copies[d].wait_recv()
        if i == 3:
            for d in range(n):
                f_copies[d].wait_recv()
        wg_copies[i].wait()
        wu_copies[i].wait()
        left = x_all[j, :, :share]
        for m in range(hidden_width // chunk):
            columns = pl.ds(m * chunk, chunk)
            gate_term = jnp.dot(left, wg_b[i, :, columns], preferred_element_type=f32)
            up_term = jnp.dot(left, wu_b[i, :, columns], preferred_element_type=f32)
            if i == 0:
                acc_g[:, columns] = gate_term
                acc_u[:, columns] = up_term
            else:
                acc_g[:, columns] += gate_term
                acc_u[:, columns] += up_term
        wide_left = left.astype(f32)
        mean_sum = mean_sum + column_of(x_all[j, :, share:])
        for e in range(experts):
            weights = router_b[e : e + 1, part(j)].astype(f32)
            scores[e] = scores[e] + jnp.sum(wide_left * weights, axis=1, keepdims=True)

    for copy in facts_copies:
        copy.wait_recv()
    facts = facts_b[...]
    scale = lax.rsqrt(mean_sum / width + EPSILON)
    pick_a, pick_b = facts[:, 0:1], facts[:, 1:2]
    gap = jnp.zeros_like(scale)
    for e in range(experts):
        gap = gap + jnp.where(pick_a == e, scores[e], 0.0) - jnp.where(pick_b == e, scores[e], 0.0)
    gap = gap * scale
    mine = (z // (n // experts)).astype(f32)
    share_of = jnp.where(pick_a == mine, jax.nn.sigmoid(gap), 0.0) + jnp.where(
        pick_b == mine, jax.nn.sigmoid(-gap), 0.0
    )
    share_of = share_of * (1.0 - facts[:, 2:3])

    def mover_of(entries, first_step_rows):
        count = entries.shape[0]
        field = lax.broadcasted_iota(jnp.int32, (n * tokens, 128), 1)
        picker = jnp.where(field == 3, 1.0, 0.0).astype(bf16)
        slots = lax.dot_general(
            picker, entries.astype(bf16), (((1,), (1,)), ((), ())), preferred_element_type=f32
        )
        place = lax.broadcasted_iota(jnp.int32, (n * tokens, count), 0)
        source = lax.broadcasted_iota(jnp.int32, (n * tokens, count), 1)
        same = (place // rows) % STEPS == (source // rows) % STEPS
        slot = (place // tokens * rows + place % rows).astype(f32)
        return jnp.where(same & (slots == slot), 1.0, 0.0).astype(bf16)

    mover = mover_of(facts, None)
    for m in range(hidden_width // chunk):
        columns = pl.ds(m * chunk, chunk)
        gate_pre = acc_g[:, columns] * scale
        upward = acc_u[:, columns] * scale
        hidden = (gate_pre * jax.nn.sigmoid(gate_pre) * upward * share_of).astype(bf16)
        hid_b[:, columns] = jnp.dot(mover, hidden, preferred_element_type=f32).astype(bf16)

    def lower(i, y):
        wd_copies[i].wait()
        return jnp.dot(hid_b[...], wd_b[i], preferred_element_type=f32)

    d_copies = [
        remote(d_send.at[i], d_recv.at[i], d_ss.at[i], d_rs.at[i], where)
        for i, where in enumerate((sibling, sibling, opposite))
    ]
    for i in range(2):
        d_send[i] = lower(i, None).astype(bf16)
        d_copies[i].start()
    value = lower(2, None)
    d_copies[0].wait_recv()
    d_send[2] = (value + d_recv[0].astype(f32)).astype(bf16)
    d_copies[2].start()
    value = lower(3, None)
    own_facts = facts_b[row_part(z), :]
    own_mover = mover_of(own_facts, None)
    kept_mix = mix_b[...] * (1.0 - own_facts[:, 2:3])
    mix_high = kept_mix.astype(bf16)
    mix_low = (kept_mix - mix_high.astype(f32)).astype(bf16)
    value = value + jnp.dot(own_mover, mix_high, preferred_element_type=f32)
    value = value + jnp.dot(own_mover, mix_low, preferred_element_type=f32)
    d_copies[1].wait_recv()
    value = value + d_recv[1].astype(f32)
    d_copies[2].wait_recv()
    value = value + d_recv[2].astype(f32)
    y_b[...] = value
    y_send[...] = value.astype(bf16)
    y_copies = []
    for d in range(1, n):
        there = lax.rem(z + d, n)
        copy = remote(
            y_send.at[row_part(there), :], y_recv.at[d - 1], y_ss.at[d - 1], y_rs.at[d - 1],
            {"row": there},
        )
        copy.start()
        y_copies.append(copy)
    total = y_b[row_part(z), :]
    for d in range(1, n):
        y_copies[d - 1].wait_recv()
        total = total + y_recv[d - 1].astype(f32)
    out_ref[...] = total.astype(bf16)
    for copy in (
        facts_copies + a_copies + z_copies + x_copies + s_copies + f_copies + d_copies + y_copies
    ):
        copy.wait_send()


def fused_local(
    prior_state,
    queries,
    new_keys,
    new_values,
    out_gates,
    decay_rates,
    norm_gain,
    out_weight,
    residual,
    ffn_gain,
    router_weight,
    gate_weight,
    up_weight,
    down_weight,
    expert_picks,
    finished,
    dest_slots,
):
    f32, bf16 = jnp.float32, jnp.bfloat16
    n = lax.axis_size("row")
    rows, heads, key_dim = queries.shape[1:]
    wide = new_values.shape[3]
    width = residual.shape[2]
    share = width // 4
    experts = router_weight.shape[1]
    hidden = gate_weight.shape[1]
    tokens = STEPS * rows
    flat = tokens * heads
    lane = lax.broadcasted_iota(jnp.int32, (STEPS, rows, 128), 2)
    facts = jnp.zeros((STEPS, rows, 128), jnp.int32)
    fields = (expert_picks[:, :, 0], expert_picks[:, :, 1], finished, dest_slots)
    for index, field in enumerate(fields):
        facts = jnp.where(lane == index, field[:, :, None], facts)
    facts = facts.astype(f32).reshape(tokens, 128)
    any_space = pl.BlockSpec(memory_space=pl.ANY)
    dma = pltpu.SemaphoreType.DMA
    out = pl.pallas_call(
        functools.partial(fused_kernel, n, experts),
        out_shape=jax.ShapeDtypeStruct((tokens, share), bf16),
        in_specs=[pl.BlockSpec(memory_space=pltpu.SMEM)] + [any_space] * 14,
        out_specs=pl.BlockSpec(memory_space=pltpu.VMEM),
        scratch_shapes=[
            pltpu.VMEM((flat, key_dim), bf16),
            pltpu.VMEM((flat, key_dim), bf16),
            pltpu.VMEM((flat, wide), bf16),
            pltpu.VMEM((flat, wide), bf16),
            pltpu.VMEM((heads, wide), f32),
            pltpu.VMEM((tokens, share), bf16),
            pltpu.VMEM((1, share), f32),
            pltpu.VMEM((experts, width), bf16),
            pltpu.VMEM((rows, heads, wide, key_dim), f32),
            pltpu.VMEM((4, heads * wide, share), bf16),
            pltpu.VMEM((4, share, hidden), bf16),
            pltpu.VMEM((4, share, hidden), bf16),
            pltpu.VMEM((4, hidden, share), bf16),
            pltpu.VMEM((flat, key_dim), f32),
            pltpu.VMEM((flat, key_dim), f32),
            pltpu.VMEM((flat, wide), f32),
            pltpu.VMEM((flat, wide), f32),
            pltpu.VMEM((tokens, heads * wide), bf16),
            pltpu.VMEM((n * tokens, 128), f32),
            pltpu.VMEM((tokens, share), f32),
            pltpu.VMEM((3, tokens, share + 128), bf16),
            pltpu.VMEM((3, tokens, share + 128), bf16),
            pltpu.VMEM((4, n * tokens, share + 128), bf16),
            pltpu.VMEM((n * tokens, hidden), f32),
            pltpu.VMEM((n * tokens, hidden), f32),
            pltpu.VMEM((n * tokens, hidden), bf16),
            pltpu.VMEM((3, n * tokens, share), bf16),
            pltpu.VMEM((3, n * tokens, share), bf16),
            pltpu.VMEM((n * tokens, share), f32),
            pltpu.VMEM((n * tokens, share), bf16),
            pltpu.VMEM((n - 1, tokens, share), bf16),
            dma((9,)), dma((1,)), dma((4,)), dma((4,)), dma((4,)), dma((4,)),
            dma((n - 1,)), dma((n - 1,)), dma((3,)), dma((3,)), dma((n - 1,)), dma((n - 1,)),
            dma((n,)), dma((n,)), dma((n,)), dma((n,)), dma((n,)), dma((n,)),
            dma((3,)), dma((3,)), dma((n - 1,)), dma((n - 1,)),
        ],
        compiler_params=pltpu.CompilerParams(
            collective_id=0, has_side_effects=True, vmem_limit_bytes=58 * 1024 * 1024
        ),
    )(
        decay_rates.reshape(1, heads),
        queries.reshape(flat, key_dim),
        new_keys.reshape(flat, key_dim),
        new_values.reshape(flat, wide),
        out_gates.reshape(flat, wide),
        norm_gain,
        residual.reshape(tokens, width),
        ffn_gain.reshape(1, width),
        router_weight.T,
        facts,
        jnp.swapaxes(prior_state, 2, 3),
        out_weight.reshape(heads * wide, width),
        gate_weight,
        up_weight,
        down_weight,
    )
    return out.reshape(STEPS, rows, share)


def solution(mesh):
    in_specs = (
        P(("group", "row"), "head", None, "sub"),
        P(None, ("group", "row"), "head", None),
        P(None, ("group", "row"), "head", None),
        P(None, ("group", "row"), "head", "sub"),
        P(None, ("group", "row"), "head", "sub"),
        P("head"),
        P("head", "sub"),
        P("head", "sub", None),
        P(None, ("group", "row"), None),
        P(),
        P(),
        P(None, ("row", "head", "sub")),
        P(None, ("row", "head", "sub")),
        P(("row", "head", "sub"), None),
        P(None, ("group", "row"), None),
        P(None, ("group", "row")),
        P(None, ("group", "row")),
    )
    out_specs = P(None, ("group", "row"), ("head", "sub"))
    small = mesh.shape["head"] == 2 and mesh.shape["sub"] == 2 and mesh.shape["row"] in (4, 8)
    part_program = fused_local if small else local
    return jax.shard_map(part_program, mesh=mesh, in_specs=in_specs, out_specs=out_specs, check_vma=False)
```
